256 devices in a mesh: space: 32 (over y, x, core), head: 8 (over z).
Axes of the slice: x: 4, y: 4, z: 8, core: 2. Of those that a mesh axis runs over, the one named last changes fastest.
Arguments:
- tokens: bfloat16 [16384, 3072], P('space'), may hold values from -21 to 21
- weight: bfloat16 [3072, 24, 384], P('space', 'head'), may hold values from -0.07307089 to 0.07307089
- grad_out: bfloat16 [16384, 3072], P('space', 'head'), may hold values from -6 to 6
- neighbours: int32 [128, 4], P('space'), may hold values from 0 to 127, as said below
Outputs:
- attended: bfloat16 [16384, 3072], P('space', 'head')
- grad_input: bfloat16 [16384, 3072], P('space', 'head')
- grad_weight: bfloat16 [3072, 24, 384], P('space', 'head')
The draws below stay inside these ranges and needn't reach their ends.
Inputs may be any that keep to these rules, and one draw needn't show every extreme that they name: `neighbours`: row t lists 4 different tiles: t, t + 4 and t - 4 (modulo 128), and tiles nearer than 4 to t modulo 128.
All inputs are finite; a program needn't handle non-finite values.
Results may differ from the reference program's by a relative error of at most 0.025.
The reference program's roundings to bfloat16 on the way (of `qkv`, `probs_b`, `dscores` and `dqkv`) count: a program that leaves them out, or rounds other values in their place, can miss the bound.
Values may be sent and summed in bfloat16 or wider, within the bound.
No kernel may reach another device: no remote copies, remote signals or barrier semaphores. Data moves between devices by JAX's collectives and lax.ppermute only.
A program may use at most 128 MiB of HBM per device.

```python
import jax
import jax.numpy as jnp
from jax import lax

D = 3072
HEADS = 24
HD = 128
TILE = 128
WIN = 4
TILES_DEV = 4
TILES = 128
TOK_DEV = 512
TOKENS = 16384
N_SPACE = 32
N_HEAD = 8


def draw_neighbours(key, part):
    key = jax.random.fold_in(key, 11)
    reach = TILES_DEV
    count = 2 * reach - 2
    extra = WIN - 3
    keys = jax.random.split(key, TILES)
    picks = jax.vmap(lambda single: jax.random.permutation(single, count))(keys)
    picks = picks[:, :extra].astype(jnp.int32)
    near = jnp.where(picks < reach - 1, picks - (reach - 1), picks - (reach - 1) + 1)
    fixed = jnp.broadcast_to(jnp.array([0, reach, -reach], jnp.int32), (TILES, 3))
    offsets = jnp.concatenate([fixed, near], axis=1)
    anchor = jnp.arange(TILES, dtype=jnp.int32)[:, None]
    return ((anchor + offsets) % TILES).astype(jnp.int32)


def draw_tokens(key, part):
    key = jax.random.fold_in(key, 21)
    base_key = jax.random.fold_in(key, 0)
    drawn = jnp.clip(jax.random.normal(base_key, (TOKENS, D), jnp.float32), -4.0, 4.0)
    return drawn.astype(jnp.bfloat16)


def draw_weight(key, part):
    key = jax.random.fold_in(key, 23)
    main_key = jax.random.fold_in(key, 0)
    factor = D ** (-0.5)
    drawn = jnp.clip(jax.random.normal(main_key, (D, HEADS, 3 * HD), jnp.float32), -4.0, 4.0) * factor
    return drawn.astype(jnp.bfloat16)


def steps_of(rng, dims, cuts, least, top_value):
    loudness, own = 1.0, jax.random.fold_in(rng, 6)
    for dim, shards_of in cuts:
        heights = jnp.exp(jax.random.uniform(jax.random.fold_in(own, dim), (shards_of,), jnp.float32, least / len(cuts), top_value / len(cuts)))
        loudness = loudness * jnp.repeat(heights, dims[dim] // shards_of).reshape([-1 if axis == dim else 1 for axis in range(len(dims))])
    return loudness


def normal_values(key, shape, scale, most, pieces=(), kind=jnp.bfloat16):
    result = scale * jax.random.normal(key, shape, jnp.float32)
    if pieces:
        result = result * steps_of(key, shape, pieces, -0.22, 0.18)
    return jnp.clip(result, -most, most).astype(kind)


def setup_inputs(seed: int = 0) -> dict:
    arg_keys = jax.random.split(jax.random.key(seed), 5)
    tokens = draw_tokens(jax.random.fold_in(arg_keys[4], 71), 0)
    weight = draw_weight(jax.random.fold_in(arg_keys[4], 71), 0)
    grad_out = normal_values(arg_keys[2], (TOKENS, HEADS * HD), 1.0, 6.0, ((0, 32), (1, 8)))
    neighbours = draw_neighbours(jax.random.fold_in(arg_keys[4], 71), 0)
    return dict(tokens=tokens, weight=weight, grad_out=grad_out, neighbours=neighbours)


def rounded(value):
    return lax.optimization_barrier(value.astype(jnp.bfloat16)).astype(jnp.float32)


def reference(tokens, weight, grad_out, neighbours):
    scale = HD ** -0.5
    qkv = jnp.einsum("td,dhe->the", tokens.astype(jnp.float32), weight.astype(jnp.float32)).astype(jnp.bfloat16)
    tiles = qkv.reshape(TILES, TILE, HEADS, 3 * HD)
    douts = grad_out.reshape(TILES, TILE, HEADS, HD)

    def one_head(head):
        block = lax.dynamic_index_in_dim(tiles, head, 2, keepdims=False)
        dout = lax.dynamic_index_in_dim(douts, head, 2, keepdims=False).astype(jnp.float32)
        query = block[:, :, :HD].astype(jnp.float32)
        keys = block[:, :, HD:2 * HD][neighbours].reshape(TILES, WIN * TILE, HD).astype(jnp.float32)
        values = block[:, :, 2 * HD:][neighbours].reshape(TILES, WIN * TILE, HD).astype(jnp.float32)
        scores = jnp.einsum("tqd,tjd->tqj", query, keys) * scale
        top = jnp.max(scores, axis=-1, keepdims=True)
        expo = jnp.exp(scores - top)
        probs = expo / jnp.sum(expo, axis=-1, keepdims=True)
        probs_b = probs.astype(jnp.bfloat16).astype(jnp.float32)
        out = jnp.einsum("tqj,tjd->tqd", probs_b, values).astype(jnp.bfloat16)
        dprobs = jnp.einsum("tqd,tjd->tqj", dout, values)
        delta = jnp.sum(probs * dprobs, axis=-1, keepdims=True)
        dscores = (probs * (dprobs - delta) * scale).astype(jnp.bfloat16).astype(jnp.float32)
        dquery = jnp.einsum("tqj,tjd->tqd", dscores, keys).astype(jnp.bfloat16)
        dkeys = jnp.einsum("tqj,tqd->tjd", dscores, query).reshape(TILES, WIN, TILE, HD)
        dvalues = jnp.einsum("tqj,tqd->tjd", probs_b, dout).reshape(TILES, WIN, TILE, HD)
        empty = jnp.zeros((TILES, TILE, HD), jnp.float32)
        dkey_sum = empty.at[neighbours].add(dkeys).astype(jnp.bfloat16)
        dvalue_sum = empty.at[neighbours].add(dvalues).astype(jnp.bfloat16)
        return out, jnp.concatenate([dquery, dkey_sum, dvalue_sum], axis=-1)

    outs, grads = lax.map(one_head, jnp.arange(HEADS))
    attended = jnp.transpose(outs, (1, 2, 0, 3)).reshape(TOKENS, HEADS * HD)
    dqkv = jnp.transpose(grads, (1, 2, 0, 3)).reshape(TOKENS, HEADS, 3 * HD)
    group = HEADS // N_HEAD
    total = jnp.zeros((TOKENS, D), jnp.float32)
    for index in range(N_HEAD):
        part = jnp.einsum("the,dhe->td", dqkv[:, index * group:(index + 1) * group].astype(jnp.float32), weight[:, index * group:(index + 1) * group].astype(jnp.float32))
        total = total + rounded(part)
    grad_input = total.astype(jnp.bfloat16)
    token_blocks = tokens.reshape(N_SPACE, TOK_DEV, D)
    grad_blocks = dqkv.reshape(N_SPACE, TOK_DEV, HEADS, 3 * HD)

    def add_block(carry, pair):
        part = jnp.einsum("tc,the->che", pair[0].astype(jnp.float32), pair[1].astype(jnp.float32))
        return carry + rounded(part), None

    summed, unused = lax.scan(add_block, jnp.zeros((D, HEADS, 3 * HD), jnp.float32), (token_blocks, grad_blocks))
    return attended, grad_input, summed.astype(jnp.bfloat16)
```

```python
import functools

import jax
import jax.numpy as jnp
from jax import lax
from jax.experimental import pallas as pl
from jax.experimental.pallas import tpu as pltpu
from jax.sharding import PartitionSpec as P

HD = 128
TILE = 128
WIN = 4
NX = 4
NY = 4
BF = jnp.bfloat16
F32 = jnp.float32
VMEM_LIMIT = 56 * 1024 * 1024


def space_perm(dy, dx, dc):
    pairs = []
    for y in range(NY):
        for x in range(NX):
            for c in range(2):
                target = (((y + dy) % NY) * NX + (x + dx) % NX) * 2 + (c ^ dc)
                pairs.append(((y * NX + x) * 2 + c, target))
    return pairs


def send(x, dy=0, dx=0, dc=0):
    return lax.ppermute(x, "space", space_perm(dy, dx, dc))


def ring(x, by):
    peers = lax.axis_size("space")
    return lax.ppermute(x, "space", [(i, (i + by) % peers) for i in range(peers)])


SLOTS = (0, -1, 1, 2)


def gather_rows(shard):
    half = shard.shape[0] // 2
    a, b = shard[:half], shard[half:]
    a4 = jnp.concatenate([a, send(a, dx=1), send(a, dx=-1), send(a, dx=2)], axis=0)
    b4 = jnp.concatenate([b, send(b, dy=1), send(b, dy=-1), send(b, dy=2)], axis=0)
    a4, b4 = lax.optimization_barrier((a4, b4))
    own = [a4, send(a4, dy=1), send(a4, dy=-1), send(a4, dy=2)]
    own += [b4, send(b4, dx=1), send(b4, dx=-1), send(b4, dx=2)]
    return own + [send(block, dc=1) for block in own]


def gather_order(y, x, c, size):
    rows = []
    for core in (c, 1 - c):
        for dy in SLOTS:
            for dx in SLOTS:
                rows.append(2 * size * ((((y + dy) % NY) * NX + (x + dx) % NX) * 2 + core))
        for dx in SLOTS:
            for dy in SLOTS:
                rows.append(2 * size * ((((y + dy) % NY) * NX + (x + dx) % NX) * 2 + core) + size)
    return rows


def add4(parts):
    return sum(part.astype(F32) for part in parts).astype(BF)


def scatter_rows(own, other):
    total = (own.astype(F32) + send(other, dc=1).astype(F32)).astype(BF)
    half = total.shape[0] // 2
    block, piece = half // 4, half // 16
    a = [total[i * block : (i + 1) * block] for i in range(4)]
    b = [total[half + i * block : half + (i + 1) * block] for i in range(4)]
    a1 = add4([a[0], send(a[1], dy=1), send(a[2], dy=-1), send(a[3], dy=2)])
    b1 = add4([b[0], send(b[1], dx=1), send(b[2], dx=-1), send(b[3], dx=2)])
    a = [a1[i * piece : (i + 1) * piece] for i in range(4)]
    b = [b1[i * piece : (i + 1) * piece] for i in range(4)]
    a2 = add4([a[0], send(a[1], dx=1), send(a[2], dx=-1), send(a[3], dx=2)])
    b2 = add4([b[0], send(b[1], dy=1), send(b[2], dy=-1), send(b[3], dy=2)])
    return jnp.concatenate([a2, b2], axis=0)


TARGETS = (0, 1, -1, 2)


def scatter_order(y, x, c, size):
    rows = []
    for core in (c, 1 - c):
        for dy in TARGETS:
            for dx in TARGETS:
                rows.append(2 * size * ((((y + dy) % NY) * NX + (x + dx) % NX) * 2 + core))
        for dx in TARGETS:
            for dy in TARGETS:
                rows.append(2 * size * ((((y + dy) % NY) * NX + (x + dx) % NX) * 2 + core) + size)
    return rows


def proj_body(blocks, size, rows_ref, tok_ref, *refs):
    pieces = refs[:blocks]
    out_ref, whole_ref, held, sem_in, sem_out = refs[blocks:]
    per = pieces[0].shape[0] // size
    for i, piece in enumerate(pieces):
        for j in range(per):
            row = pl.multiple_of(rows_ref[i * per + j], size)
            pltpu.make_async_copy(
                piece.at[pl.ds(j * size, size)], held.at[pl.ds(row, size)], sem_in
            ).start()
    pltpu.make_async_copy(whole_ref, held, sem_in).wait()
    back = pltpu.make_async_copy(held, whole_ref, sem_out)
    back.start()
    step = 384

    @pl.loop(0, held.shape[1] // step)
    def _(i):
        cols = pl.ds(pl.multiple_of(i * step, step), step)
        out_ref[:, cols] = jnp.dot(
            tok_ref[...], held[:, cols], preferred_element_type=F32
        ).astype(BF)

    back.wait()


def project_pieces(rows, tokens, pieces, size):
    depth, width = tokens.shape[1], pieces[0].shape[1]
    vmem = pl.BlockSpec(memory_space=pltpu.VMEM)
    hbm = pl.BlockSpec(memory_space=pl.ANY)
    return pl.pallas_call(
        functools.partial(proj_body, len(pieces), size),
        out_shape=[
            jax.ShapeDtypeStruct((tokens.shape[0], width), BF),
            jax.ShapeDtypeStruct((depth, width), BF),
        ],
        in_specs=[pl.BlockSpec(memory_space=pltpu.SMEM), vmem] + [hbm] * len(pieces),
        out_specs=[vmem, hbm],
        scratch_shapes=[
            pltpu.VMEM((depth, width), BF),
            pltpu.SemaphoreType.DMA,
            pltpu.SemaphoreType.DMA,
        ],
        compiler_params=pltpu.CompilerParams(vmem_limit_bytes=VMEM_LIMIT),
        cost_estimate=pl.CostEstimate(
            flops=2 * tokens.shape[0] * depth * width,
            bytes_accessed=2 * (tokens.size + 2 * depth * width),
            transcendentals=0,
        ),
        name="project_pieces",
    )(rows, tokens, *pieces)


def attention_body(heads, tiles, places_ref, q_ref, kv_ref, left_ref, right_ref, dout_ref,
                   att_ref, dq_ref, own_ref, dleft_ref, dright_ref, ext, acc, sem):
    rows = tiles * TILE
    scale = HD ** (-0.5)
    copies = []
    for i, ref in enumerate((left_ref, kv_ref, right_ref)):
        copy = pltpu.make_async_copy(ref, ext.at[pl.ds(i * rows, rows)], sem.at[i])
        copy.start()
        copies.append(copy)
    acc[...] = jnp.zeros_like(acc)
    for copy in copies:
        copy.wait()

    def tile(t, carry):
        here = pl.ds(pl.multiple_of(t * TILE, TILE), TILE)
        window = [
            pl.ds(pl.multiple_of(places_ref[t * WIN + w] * TILE, TILE), TILE) for w in range(WIN)
        ]
        for h in range(heads):
            kcol = pl.ds(h * HD, HD)
            vcol = pl.ds((heads + h) * HD, HD)
            query = q_ref[here, kcol]
            dout = dout_ref[here, kcol]
            keys = jnp.concatenate([ext[rng, kcol] for rng in window], axis=0)
            values = jnp.concatenate([ext[rng, vcol] for rng in window], axis=0)
            nt = (((1,), (1,)), ((), ()))
            tn = (((0,), (0,)), ((), ()))
            scores = lax.dot_general(keys, query, nt, preferred_element_type=F32) * scale
            expo = jnp.exp(scores - jnp.max(scores, axis=0, keepdims=True))
            probs = expo / jnp.sum(expo, axis=0, keepdims=True)
            probs_b = probs.astype(BF)
            dprobs = lax.dot_general(values, dout, nt, preferred_element_type=F32)
            delta = jnp.sum(probs * dprobs, axis=0, keepdims=True)
            dscores = (probs * (dprobs - delta) * scale).astype(BF)
            att_ref[here, kcol] = lax.dot_general(
                probs_b, values, tn, preferred_element_type=F32
            ).astype(BF)
            dq_ref[here, kcol] = lax.dot_general(
                dscores, keys, tn, preferred_element_type=F32
            ).astype(BF)
            dkeys = jnp.dot(dscores, query, preferred_element_type=F32)
            dvalues = jnp.dot(probs_b, dout, preferred_element_type=F32)
            for w, rng in enumerate(window):
                acc[rng, kcol] += dkeys[w * TILE : (w + 1) * TILE]
                acc[rng, vcol] += dvalues[w * TILE : (w + 1) * TILE]
        return carry

    lax.fori_loop(0, tiles, tile, 0)
    dleft_ref[...] = acc[pl.ds(0, rows)].astype(BF)
    own_ref[...] = acc[pl.ds(rows, rows)]
    dright_ref[...] = acc[pl.ds(2 * rows, rows)].astype(BF)


def attention(places, query, kv, left, right, dout):
    rows, width = query.shape
    heads, tiles = width // HD, rows // TILE
    vmem = pl.BlockSpec(memory_space=pltpu.VMEM)
    hbm = pl.BlockSpec(memory_space=pl.ANY)
    return pl.pallas_call(
        functools.partial(attention_body, heads, tiles),
        out_shape=[
            jax.ShapeDtypeStruct((rows, width), BF),
            jax.ShapeDtypeStruct((rows, width), BF),
            jax.ShapeDtypeStruct((rows, 2 * width), F32),
            jax.ShapeDtypeStruct((rows, 2 * width), BF),
            jax.ShapeDtypeStruct((rows, 2 * width), BF),
        ],
        in_specs=[pl.BlockSpec(memory_space=pltpu.SMEM), vmem, hbm, hbm, hbm, vmem],
        out_specs=[vmem] * 5,
        scratch_shapes=[
            pltpu.VMEM((3 * rows, 2 * width), BF),
            pltpu.VMEM((3 * rows, 2 * width), F32),
            pltpu.SemaphoreType.DMA((3,)),
        ],
        compiler_params=pltpu.CompilerParams(vmem_limit_bytes=VMEM_LIMIT),
        cost_estimate=pl.CostEstimate(
            flops=12 * rows * WIN * TILE * width,
            bytes_accessed=12 * rows * width * 2,
            transcendentals=rows * WIN * TILE * heads,
        ),
        name="attention",
    )(places, query, kv, left, right, dout)


def wgrad_body(size, groups, rows_ref, tok_ref, d_ref, own_ref, other_ref, held, sem):
    i = pl.program_id(0)
    slot = lax.rem(i, 2)
    per = held.shape[1] // size

    def wait(at):
        pltpu.make_async_copy(held.at[at], own_ref.at[pl.ds(0, held.shape[1])], sem.at[at]).wait()

    @pl.when(i >= 2)
    def _():
        wait(slot)

    held[slot] = jnp.dot(tok_ref[...], d_ref[...], preferred_element_type=F32).astype(BF)
    for j in range(per):
        core = (j // 2) % 2
        row = pl.multiple_of(rows_ref[i * per + j], size)
        src = held.at[slot, pl.ds(j * size, size)]
        mine = rows_ref[groups * per] == core

        @pl.when(mine)
        def _():
            pltpu.make_async_copy(src, own_ref.at[pl.ds(row, size)], sem.at[slot]).start()

        @pl.when(jnp.logical_not(mine))
        def _():
            pltpu.make_async_copy(src, other_ref.at[pl.ds(row, size)], sem.at[slot]).start()

    @pl.when(i == groups - 1)
    def _():
        wait(1 - slot)
        wait(slot)


def weight_grad(rows, tok_t, dpart, size):
    depth, tokens = tok_t.shape
    width = dpart.shape[1]
    groups = NY
    chunk = depth // groups
    hbm = pl.BlockSpec(memory_space=pl.ANY)
    return pl.pallas_call(
        functools.partial(wgrad_body, size, groups),
        grid=(groups,),
        out_shape=[jax.ShapeDtypeStruct((depth // 2, width), BF)] * 2,
        in_specs=[
            pl.BlockSpec(memory_space=pltpu.SMEM),
            pl.BlockSpec((chunk, tokens), lambda i: (i, 0)),
            pl.BlockSpec((tokens, width), lambda i: (0, 0)),
        ],
        out_specs=[hbm, hbm],
        scratch_shapes=[pltpu.VMEM((2, chunk, width), BF), pltpu.SemaphoreType.DMA((2,))],
        compiler_params=pltpu.CompilerParams(vmem_limit_bytes=VMEM_LIMIT),
        cost_estimate=pl.CostEstimate(
            flops=2 * depth * tokens * width,
            bytes_accessed=2 * (depth * tokens + depth * width),
            transcendentals=0,
        ),
        name="weight_grad",
    )(rows, tok_t, dpart)


def input_grad_body(dkv_ref, dq_ref, wkv_ref, wq_ref, out_ref):
    nt = (((1,), (1,)), ((), ()))
    total = lax.dot_general(dkv_ref[...], wkv_ref[...], nt, preferred_element_type=F32)
    total += lax.dot_general(dq_ref[...], wq_ref[...], nt, preferred_element_type=F32)
    out_ref[0] = total.astype(BF)


def input_grad(dkv, dq, w_kv, w_q, parts):
    rows, depth = dkv.shape[0], w_kv.shape[0]
    chunk = depth // parts
    return pl.pallas_call(
        input_grad_body,
        grid=(parts,),
        out_shape=jax.ShapeDtypeStruct((parts, rows, chunk), BF),
        in_specs=[
            pl.BlockSpec(dkv.shape, lambda i: (0, 0)),
            pl.BlockSpec(dq.shape, lambda i: (0, 0)),
            pl.BlockSpec((chunk, w_kv.shape[1]), lambda i: (i, 0)),
            pl.BlockSpec((chunk, w_q.shape[1]), lambda i: (i, 0)),
        ],
        out_specs=pl.BlockSpec((1, rows, chunk), lambda i: (i, 0, 0)),
        compiler_params=pltpu.CompilerParams(vmem_limit_bytes=VMEM_LIMIT),
        cost_estimate=pl.CostEstimate(
            flops=2 * rows * depth * (dkv.shape[1] + dq.shape[1]),
            bytes_accessed=2 * (w_kv.size + w_q.size + rows * depth),
            transcendentals=0,
        ),
        name="input_grad",
    )(dkv, dq, w_kv, w_q)


def shards(tokens, weight, grad_out, neighbours):
    rows, depth = tokens.shape
    owned, heads = weight.shape[:2]
    size = owned // 2
    tiles = rows // TILE
    tiles_all = tiles * lax.axis_size("space")
    index = lax.axis_index("space")
    c, x, y = index % 2, (index // 2) % NX, index // (2 * NX)

    split = weight.reshape(owned, heads, 3, HD)
    w_kv = split[:, :, 1:].transpose(0, 2, 1, 3).reshape(owned, 2 * heads * HD)
    w_q = split[:, :, 0].reshape(owned, heads * HD)
    w_kv, w_q = lax.optimization_barrier((w_kv, w_q))

    order = jnp.stack(gather_order(y, x, c, size)).astype(jnp.int32)
    pieces = gather_rows(w_kv)
    kv, whole_kv = project_pieces(order, tokens, pieces, size)
    left, right = ring(kv, 1), ring(kv, -1)
    query, whole_q = project_pieces(order, tokens, gather_rows(w_q), size)

    own = jnp.arange(tiles, dtype=jnp.int32)[:, None]
    offsets = (neighbours - (index * tiles + own) + tiles) % tiles_all - tiles
    places = (own + tiles + offsets).reshape(-1)
    attended, dq, dkv_own, dleft, dright = attention(places, query, kv, left, right, grad_out)
    from_right, from_left = ring(dleft, -1), ring(dright, 1)

    starts = jnp.stack(scatter_order(y, x, c, size)).astype(jnp.int32) // size
    count = starts.shape[0]
    where = jnp.zeros((count,), jnp.int32).at[starts].set(jnp.arange(count, dtype=jnp.int32))
    where = (where % (count // 2)) * size
    where = jnp.concatenate([where, c[None].astype(jnp.int32)])
    tok_t = tokens.T

    gq = scatter_rows(*weight_grad(where, tok_t, dq, size))
    dkv = (dkv_own + from_right.astype(F32) + from_left.astype(F32)).astype(BF)
    gkv = scatter_rows(*weight_grad(where, tok_t, dkv, size))
    term = input_grad(dkv, dq, whole_kv, whole_q, lax.axis_size("head"))
    grad_input = lax.psum_scatter(term, "head", scatter_dimension=0, tiled=True)[0]

    grad_weight = jnp.concatenate(
        [gq.reshape(owned, heads, 1, HD), gkv.reshape(owned, 2, heads, HD).transpose(0, 2, 1, 3)],
        axis=2,
    ).reshape(weight.shape)
    return (attended, grad_input, grad_weight)


def solution(mesh):
    return jax.shard_map(
        shards,
        mesh=mesh,
        in_specs=(P("space", None), P("space", "head", None), P("space", "head"), P("space", None)),
        out_specs=(P("space", "head"), P("space", "head"), P("space", "head", None)),
        check_vma=False,
    )
```

```python
import functools

import jax
import jax.numpy as jnp
from jax import lax
from jax.experimental import pallas as pl
from jax.experimental.pallas import tpu as pltpu
from jax.sharding import PartitionSpec as P

HD = 128
TILE = 128
WIN = 4
NX = 4
NY = 4
BF = jnp.bfloat16
F32 = jnp.float32
VMEM_LIMIT = 56 * 1024 * 1024


def space_perm(move):
    pairs = []
    for y in range(NY):
        for x in range(NX):
            for c in range(2):
                to_y, to_x, to_c = move(y, x, c)
                pairs.append(((y * NX + x) * 2 + c, (to_y % NY * NX + to_x % NX) * 2 + to_c))
    return pairs


def permute(value, move):
    return lax.ppermute(value, "space", space_perm(move))


def swap(value):
    return permute(value, lambda y, x, c: (y, x, 1 - c))


def minor(value, by):
    return permute(value, lambda y, x, c: (y + by * c, x + by * (1 - c), c))


def major(value, by):
    return permute(value, lambda y, x, c: (y + by * (1 - c), x + by * c, c))


def outside(value):
    peers = lax.axis_size("space")
    return lax.ppermute(
        value, "space", [(i, (i + 1 if i % 2 else i - 1) % peers) for i in range(peers)]
    )


NEAR = (0, -1, 1, 2)


def block_order(y, x, c, owned):
    groups = (
        [(0, q) for q in NEAR],
        [(-1, q) for q in NEAR[:2]] + [(1, q) for q in NEAR[2:]],
        [(-1, q) for q in NEAR[2:]] + [(1, q) for q in NEAR[:2]],
        [(2, q) for q in NEAR],
    )
    rows = []
    for group in groups:
        for core in (c, 1 - c):
            for p, q in group:
                dy = jnp.where(core == 0, p, q)
                dx = jnp.where(core == 0, q, p)
                rows.append(((((y + dy) % NY) * NX + (x + dx) % NX) * 2 + core) * owned)
    return jnp.stack(rows).astype(jnp.int32)


def gather_rows(shard, tok_t, project_early):
    h0 = jnp.concatenate([shard, minor(shard, 1)], axis=0)
    h1 = jnp.concatenate([minor(shard, -1), minor(shard, 2)], axis=0)
    h0, h1, tok_t = lax.optimization_barrier((h0, h1, tok_t))
    r0, l1 = major(h0, 1), major(h1, -1)
    r1, l0 = major(h1, 1), major(h0, -1)
    near = jnp.concatenate([h0, h1], axis=0)
    first = jnp.concatenate([r0, l1], axis=0)
    f0, f1 = major(r0, 1), major(l1, -1)
    second = jnp.concatenate([r1, l0], axis=0)
    early = [near, swap(near), first, swap(first), second, swap(second)]
    part = project_early(tok_t, early)
    f0, f1, part = lax.optimization_barrier((f0, f1, part))
    far = jnp.concatenate([f0, f1], axis=0)
    return tok_t, part, early + [far, swap(far)]


def add(*parts):
    return sum(part.astype(F32) for part in parts).astype(BF)


def scatter_rows(here, first, second, far):
    def halves(group):
        h0, h1, other = group
        got = swap(other)
        cut = h0.shape[0]
        return (h0, got[:cut]), (h1, got[cut:])

    far0, far1 = halves(far)
    g0, g1 = major(add(*far0), 1), major(add(*far1), -1)
    left0, right1 = halves(first)
    t0, t1 = major(add(*left0), -1), major(add(*right1), 1)
    left1, right0 = halves(second)
    u0, u1 = major(add(*right0, g0), 1), major(add(*left1, g1), -1)
    here0, here1 = halves(here)
    owned = u0.shape[0] // 2

    def part(rng, *parts):
        return add(*[value[rng] for value in parts])

    first, second = slice(0, owned), slice(owned, 2 * owned)
    n1 = minor(part(second, *here0, t0, u0), -1)
    n2 = minor(part(first, *here1, t1, u1), 1)
    n3 = minor(part(second, *here1, t1, u1), 2)
    return add(*[value[first] for value in (*here0, t0, u0)], n1, n2, n3)


def weight_rows_body(starts, size, rows_ref, *refs):
    pieces, (out_ref, sem) = refs[:-2], refs[-2:]
    for i, piece in enumerate(pieces):
        for j in range(piece.shape[0] // size):
            row = pl.multiple_of(rows_ref[starts[i] // size + j], size)
            pltpu.make_async_copy(
                piece.at[pl.ds(j * size, size)], out_ref.at[pl.ds(row, size)], sem
            ).start()
    pltpu.make_async_copy(out_ref, out_ref, sem).wait()


def weight_rows(order, pieces, size):
    starts, depth = [], 0
    for piece in pieces:
        starts.append(depth)
        depth += piece.shape[0]
    width = pieces[0].shape[1]
    hbm = pl.BlockSpec(memory_space=pl.ANY)
    return pl.pallas_call(
        functools.partial(weight_rows_body, tuple(starts), size),
        out_shape=jax.ShapeDtypeStruct((depth, width), BF),
        in_specs=[pl.BlockSpec(memory_space=pltpu.SMEM)] + [hbm] * len(pieces),
        out_specs=pl.BlockSpec(memory_space=pltpu.VMEM),
        scratch_shapes=[pltpu.SemaphoreType.DMA],
        compiler_params=pltpu.CompilerParams(vmem_limit_bytes=VMEM_LIMIT),
        cost_estimate=pl.CostEstimate(
            flops=0, bytes_accessed=4 * depth * width, transcendentals=0
        ),
        name="weight_rows",
    )(order, *pieces)


TN = (((0,), (0,)), ((), ()))
NT = (((1,), (1,)), ((), ()))


def load(pieces, rows_ref, first, size, tok_ref, weight, tok, sems):
    parts, start = [], 0
    for i, piece in enumerate(pieces):
        count = piece.shape[0]
        rng = pl.ds(start, count)
        pltpu.make_async_copy(piece, weight.at[rng], sems.at[0, i]).start()
        for j in range(count // size):
            row = pl.multiple_of(rows_ref[first + start // size + j], size)
            pltpu.make_async_copy(
                tok_ref.at[pl.ds(row, size)], tok.at[pl.ds(start + j * size, size)], sems.at[1, i]
            ).start()
        waits = (
            pltpu.make_async_copy(piece, weight.at[rng], sems.at[0, i]),
            pltpu.make_async_copy(tok_ref.at[pl.ds(0, count)], tok.at[rng], sems.at[1, i]),
        )
        parts.append((rng, waits))
        start += count
    return parts


def early_body(count, size, rows_ref, tok_ref, *refs):
    pieces, (out_ref, weight, tok, sems) = refs[:count], refs[count:]
    parts = load(pieces, rows_ref, 0, size, tok_ref, weight, tok, sems)
    for i in range(0, count, 2):
        for _, waits in parts[i : i + 2]:
            for wait in waits:
                wait.wait()
        start, rows = parts[i][0].start, sum(piece.shape[0] for piece in pieces[i : i + 2])
        total = lax.dot_general(
            tok[start : start + rows, :],
            weight[start : start + rows, :],
            TN,
            preferred_element_type=F32,
        )
        out_ref[...] = total if i == 0 else out_ref[...] + total


def late_body(first, count, size, rows_ref, part_ref, tok_ref, *refs):
    pieces, outs, (weight, tok, sems) = refs[:count], refs[count:-3], refs[-3:]
    parts = load(pieces, rows_ref, first, size, tok_ref, weight, tok, sems)
    for _, waits in parts:
        for wait in waits:
            wait.wait()
    total = lax.dot_general(tok[...], weight[...], TN, preferred_element_type=F32)
    total = (total + part_ref[...]).astype(BF)
    start = 0
    for out in outs:
        out[...] = total[:, start : start + out.shape[1]]
        start += out.shape[1]


def projection(body, order, size, tok_t, pieces, part, outs, name):
    rows, width = tok_t.shape[1], pieces[0].shape[1]
    depth = sum(piece.shape[0] for piece in pieces)
    vmem = pl.BlockSpec(memory_space=pltpu.VMEM)
    smem = pl.BlockSpec(memory_space=pltpu.SMEM)
    hbm = pl.BlockSpec(memory_space=pl.ANY)
    return pl.pallas_call(
        functools.partial(body, len(pieces), size),
        out_shape=outs,
        in_specs=[smem] + [vmem] * len(part) + [hbm] * (1 + len(pieces)),
        out_specs=[vmem] * len(outs),
        scratch_shapes=[
            pltpu.VMEM((depth, width), BF),
            pltpu.VMEM((depth, rows), BF),
            pltpu.SemaphoreType.DMA((2, len(pieces))),
        ],
        compiler_params=pltpu.CompilerParams(vmem_limit_bytes=VMEM_LIMIT),
        cost_estimate=pl.CostEstimate(
            flops=2 * rows * depth * width,
            bytes_accessed=2 * (rows + width) * depth + 4 * rows * width,
            transcendentals=0,
        ),
        name=name,
    )(order, *part, tok_t, *pieces)


def attention_body(heads, tiles, places_ref, q_ref, kv_ref, out_ref, in_ref, dout_ref,
                   att_ref, dq_ref, own_ref, dout_side_ref, din_side_ref, ext, acc, sem):
    rows = tiles * TILE
    scale = HD ** (-0.5)
    copies = []
    for i, ref in enumerate((out_ref, kv_ref, in_ref)):
        copy = pltpu.make_async_copy(ref, ext.at[pl.ds(i * rows, rows)], sem.at[i])
        copy.start()
        copies.append(copy)
    acc[...] = jnp.zeros_like(acc)
    for copy in copies:
        copy.wait()

    def tile(t, carry):
        here = pl.ds(pl.multiple_of(t * TILE, TILE), TILE)
        window = [
            pl.ds(pl.multiple_of(places_ref[t * WIN + w] * TILE, TILE), TILE) for w in range(WIN)
        ]
        for h in range(heads):
            col = pl.ds(h * HD, HD)
            kcol, vcol = pl.ds(2 * h * HD, HD), pl.ds((2 * h + 1) * HD, HD)
            query = q_ref[here, col]
            dout = dout_ref[here, col]
            keys = jnp.concatenate([ext[rng, kcol] for rng in window], axis=0)
            values = jnp.concatenate([ext[rng, vcol] for rng in window], axis=0)
            scores = lax.dot_general(keys, query, NT, preferred_element_type=F32) * scale
            expo = jnp.exp(scores - jnp.max(scores, axis=0, keepdims=True))
            probs = expo * (1.0 / jnp.sum(expo, axis=0, keepdims=True))
            probs_b = probs.astype(BF)
            dprobs = lax.dot_general(values, dout, NT, preferred_element_type=F32)
            delta = jnp.sum(probs * dprobs, axis=0, keepdims=True)
            dscores = (probs * (dprobs - delta) * scale).astype(BF)
            att_ref[here, col] = lax.dot_general(
                probs_b, values, TN, preferred_element_type=F32
            ).astype(BF)
            dq_ref[here, col] = lax.dot_general(
                dscores, keys, TN, preferred_element_type=F32
            ).astype(BF)
            dkeys = jnp.dot(dscores, query, preferred_element_type=F32)
            dvalues = jnp.dot(probs_b, dout, preferred_element_type=F32)
            for w, rng in enumerate(window):
                part = slice(w * TILE, (w + 1) * TILE)
                acc[rng, kcol] += dkeys[part]
                acc[rng, vcol] += dvalues[part]
        return carry

    lax.fori_loop(0, tiles, tile, 0)
    dout_side_ref[...] = acc[pl.ds(0, rows)].astype(BF)
    own_ref[...] = acc[pl.ds(rows, rows)]
    din_side_ref[...] = acc[pl.ds(2 * rows, rows)].astype(BF)


def attention(places, query, kv, out_side, in_side, grad_out, first):
    rows, width = kv.shape[0], kv.shape[1] // 2
    heads, tiles = width // HD, rows // TILE
    block = first // heads
    part = pl.BlockSpec((rows, width), lambda i: (0, block))
    vmem = pl.BlockSpec(memory_space=pltpu.VMEM)
    hbm = pl.BlockSpec(memory_space=pl.ANY)
    return pl.pallas_call(
        functools.partial(attention_body, heads, tiles),
        grid=(1,),
        out_shape=[
            jax.ShapeDtypeStruct((rows, width), BF),
            jax.ShapeDtypeStruct((rows, width), BF),
            jax.ShapeDtypeStruct((rows, 2 * width), F32),
            jax.ShapeDtypeStruct((rows, 2 * width), BF),
            jax.ShapeDtypeStruct((rows, 2 * width), BF),
        ],
        in_specs=[pl.BlockSpec(memory_space=pltpu.SMEM), part, hbm, hbm, hbm, part],
        out_specs=[pl.BlockSpec((rows, cols), lambda i: (0, 0)) for cols in (width, width, 2 * width, 2 * width, 2 * width)],
        scratch_shapes=[
            pltpu.VMEM((3 * rows, 2 * width), BF),
            pltpu.VMEM((3 * rows, 2 * width), F32),
            pltpu.SemaphoreType.DMA((3,)),
        ],
        compiler_params=pltpu.CompilerParams(vmem_limit_bytes=VMEM_LIMIT),
        cost_estimate=pl.CostEstimate(
            flops=24 * rows * WIN * TILE * width,
            bytes_accessed=24 * rows * width,
            transcendentals=rows * WIN * TILE * heads,
        ),
        name="attention",
    )(places, query, kv, out_side, in_side, grad_out)


def weight_grad_body(first, size, count, rows_ref, tok_ref, d_ref, *refs):
    outs, (tok, held, sems, sems_out) = refs[:count], refs[count:]
    starts, start = [], 0
    for i, out in enumerate(outs):
        for j in range(out.shape[0] // size):
            row = pl.multiple_of(rows_ref[first + start // size + j], size)
            pltpu.make_async_copy(
                tok_ref.at[pl.ds(row, size)], tok.at[pl.ds(start + j * size, size)], sems.at[i]
            ).start()
        starts.append(start)
        start += out.shape[0]
    for i, out in enumerate(outs):
        rng = pl.ds(starts[i], out.shape[0])
        pltpu.make_async_copy(tok_ref.at[pl.ds(0, out.shape[0])], tok.at[rng], sems.at[i]).wait()
        held[rng, :] = jnp.dot(tok[rng, :], d_ref[...], preferred_element_type=F32).astype(BF)
        pltpu.make_async_copy(held.at[rng], out, sems_out.at[i]).start()
    for i, out in enumerate(outs):
        rng = pl.ds(starts[i], out.shape[0])
        pltpu.make_async_copy(held.at[rng], out, sems_out.at[i]).wait()


def weight_grad(order, tok_t, dqkv, first, size, sizes):
    tokens, width = dqkv.shape
    depth = sum(sizes)
    vmem = pl.BlockSpec(memory_space=pltpu.VMEM)
    return pl.pallas_call(
        functools.partial(weight_grad_body, first, size, len(sizes)),
        out_shape=[jax.ShapeDtypeStruct((out, width), BF) for out in sizes],
        in_specs=[
            pl.BlockSpec(memory_space=pltpu.SMEM),
            pl.BlockSpec(memory_space=pl.ANY),
            vmem,
        ],
        out_specs=[pl.BlockSpec(memory_space=pl.ANY)] * len(sizes),
        scratch_shapes=[
            pltpu.VMEM((depth, tokens), BF),
            pltpu.VMEM((depth, width), BF),
            pltpu.SemaphoreType.DMA((len(sizes),)),
            pltpu.SemaphoreType.DMA((len(sizes),)),
        ],
        compiler_params=pltpu.CompilerParams(vmem_limit_bytes=VMEM_LIMIT),
        cost_estimate=pl.CostEstimate(
            flops=2 * depth * tokens * width,
            bytes_accessed=2 * (depth * tokens + depth * width),
            transcendentals=0,
        ),
        name="weight_grad",
    )(order, tok_t, dqkv)


def input_grad_body(d_ref, w_ref, out_ref):
    total = lax.dot_general(d_ref[...], w_ref[...], NT, preferred_element_type=F32).astype(BF)
    chunk = out_ref.shape[2]
    for i in range(out_ref.shape[0]):
        out_ref[i] = total[:, i * chunk : (i + 1) * chunk]


def input_grad(dqkv, whole, parts):
    rows, width = dqkv.shape
    depth = whole.shape[0]
    chunk = depth // parts
    step = 2
    return pl.pallas_call(
        input_grad_body,
        grid=(parts // step,),
        out_shape=jax.ShapeDtypeStruct((parts, rows, chunk), BF),
        in_specs=[
            pl.BlockSpec((rows, width), lambda i: (0, 0)),
            pl.BlockSpec((chunk * step, width), lambda i: (i, 0)),
        ],
        out_specs=pl.BlockSpec((step, rows, chunk), lambda i: (i, 0, 0)),
        compiler_params=pltpu.CompilerParams(vmem_limit_bytes=VMEM_LIMIT),
        cost_estimate=pl.CostEstimate(
            flops=2 * rows * depth * width,
            bytes_accessed=2 * (depth * width + rows * depth),
            transcendentals=0,
        ),
        name="input_grad",
    )(dqkv, whole)


def shards(tokens, weight, grad_out, neighbours):
    rows, depth = tokens.shape
    owned, heads = weight.shape[:2]
    size = owned // 2
    tiles = rows // TILE
    tiles_all = tiles * lax.axis_size("space")
    index = lax.axis_index("space")
    c, x, y = index % 2, (index // 2) % NX, index // (2 * NX)

    split = weight.reshape(owned, heads, 3, HD)
    flat = jnp.concatenate(
        [split[:, :, 1:].reshape(owned, -1), split[:, :, 0].reshape(owned, -1)], axis=1
    )
    order = block_order(y, x, c, owned)
    width = flat.shape[1]

    def project_early(tok_t, pieces):
        out = jax.ShapeDtypeStruct((rows, width), F32)
        return projection(early_body, order, owned, tok_t, pieces, (), [out], "project_early")[0]

    tok_t, part, pieces = gather_rows(flat, tokens.T, project_early)
    groups = ((0, heads - 1), (heads - 1, 1))
    cols = [2 * count * HD for _, count in groups] + [heads * HD]
    kv_a, kv_b, query = projection(
        functools.partial(late_body, 24), order, owned, tok_t, pieces[6:], (part,),
        [jax.ShapeDtypeStruct((rows, count), BF) for count in cols], "project_late",
    )
    whole = weight_rows(order, pieces, owned)

    places = (neighbours - (index - 1) * tiles) % tiles_all
    block = places // tiles
    places = (jnp.where(c == 0, block, 2 - block) * tiles + places % tiles).reshape(-1)
    sides = [(kv, outside(kv), swap(kv)) for kv in (kv_a, kv_b)]
    sides[0], whole = lax.optimization_barrier((sides[0], whole))
    outs, dqs, dkvs = [], [], []
    for (first, _), side in zip(groups, sides):
        out, dq, dkv, dout_side, din_side = attention(places, query, *side, grad_out, first)
        outs.append(out)
        dqs.append(dq)
        dkvs.append(add(dkv, outside(dout_side), swap(din_side)))
    attended = jnp.concatenate(outs, axis=1)
    dqkv = jnp.concatenate(dkvs + dqs, axis=1)

    unit = depth // 16
    sizes = (unit, unit, 2 * unit)
    far = weight_grad(order, tok_t, dqkv, 24, owned, sizes)
    dqkv, far = lax.optimization_barrier((dqkv, far))
    term = input_grad(dqkv, whole, lax.axis_size("head"))
    dqkv, term = lax.optimization_barrier((dqkv, term))
    grad_input = lax.psum_scatter(term, "head", scatter_dimension=0, tiled=True)[0]
    rest = weight_grad(order, tok_t, dqkv, 0, owned, sizes * 3)
    mine = scatter_rows(rest[:3], rest[3:6], rest[6:], far)
    cut = 2 * heads * HD
    grad_weight = jnp.concatenate(
        [
            mine[:, cut:].reshape(owned, heads, 1, HD),
            mine[:, :cut].reshape(owned, heads, 2, HD),
        ],
        axis=2,
    ).reshape(weight.shape)
    return (attended, grad_input, grad_weight)


def solution(mesh):
    return jax.shard_map(
        shards,
        mesh=mesh,
        in_specs=(P("space", None), P("space", "head", None), P("space", "head"), P("space", None)),
        out_specs=(P("space", "head"), P("space", "head"), P("space", "head", None)),
        check_vma=False,
    )
```

```python
import functools

import jax
import jax.numpy as jnp
from jax import lax
from jax.experimental import pallas as pl
from jax.experimental.pallas import tpu as pltpu
from jax.sharding import PartitionSpec as P

HD = 128
TILE = 128
WIN = 4
NX = 4
NY = 4
BF = jnp.bfloat16
F32 = jnp.float32
VMEM_LIMIT = 56 * 1024 * 1024
VMEM_SMALL = 28 * 1024 * 1024


def space_perm(move):
    pairs = []
    for y in range(NY):
        for x in range(NX):
            for c in range(2):
                to_y, to_x, to_c = move(y, x, c)
                pairs.append(((y * NX + x) * 2 + c, (to_y % NY * NX + to_x % NX) * 2 + to_c))
    return pairs


def permute(value, move):
    return lax.ppermute(value, "space", space_perm(move))


def swap(value):
    return permute(value, lambda y, x, c: (y, x, 1 - c))


def minor(value, by):
    return permute(value, lambda y, x, c: (y + by * c, x + by * (1 - c), c))


def major(value, by):
    return permute(value, lambda y, x, c: (y + by * (1 - c), x + by * c, c))


def outside(value):
    peers = lax.axis_size("space")
    return lax.ppermute(
        value, "space", [(i, (i + 1 if i % 2 else i - 1) % peers) for i in range(peers)]
    )


NEAR = (0, -1, 1, 2)


def ring_heads(value):
    space, peers = lax.axis_size("space"), lax.axis_size("head")
    pairs = []
    for i in range(space):
        for j in range(peers):
            pairs.append((i * peers + j, i * peers + (j + 1 - 2 * (i % 2)) % peers))
    return lax.ppermute(value, ("space", "head"), pairs)


GROUPS = (((0, 0), (0, 1)), ((-1, 0), (1, 1)), ((-1, 1), (1, 0)), ((2, 0), (2, 1)))


def block_order(y, x, c, owned):
    rows = []
    for group in GROUPS:
        for core in (c, 1 - c):
            for p, half in group:
                for q in NEAR[2 * half : 2 * half + 2]:
                    dy = jnp.where(core == 0, p, q)
                    dx = jnp.where(core == 0, q, p)
                    rows.append(((((y + dy) % NY) * NX + (x + dx) % NX) * 2 + core) * owned)
    return jnp.stack(rows).astype(jnp.int32)


def gather_rows(shard, tok_t, project_early):
    h0 = jnp.concatenate([shard, minor(shard, 1)], axis=0)
    h1 = jnp.concatenate([minor(shard, -1), minor(shard, 2)], axis=0)
    h0, h1, tok_t = lax.optimization_barrier((h0, h1, tok_t))
    r0, l1 = major(h0, 1), major(h1, -1)
    r1, l0 = major(h1, 1), major(h0, -1)
    near = jnp.concatenate([h0, h1], axis=0)
    f0, f1 = major(r0, 1), major(l1, -1)
    early = [near, swap(near), r0, l1]
    part = project_early(tok_t, early)
    r0, l1, r1, l0 = lax.optimization_barrier((r0, l1, r1, l0))
    f0, f1, part = lax.optimization_barrier((f0, f1, part))
    late = [swap(r0), swap(l1), r1, l0, swap(r1), swap(l0), f0, f1, swap(f0), swap(f1)]
    return tok_t, part, early, late


def add(*parts):
    return sum(part.astype(F32) for part in parts).astype(BF)


def scatter_rows(here, first, second, far):
    here0, here1 = here
    left0, right1 = first
    left1, right0 = second
    g0, g1 = major(far[0], 1), major(far[1], -1)
    t0, t1 = major(left0, -1), major(right1, 1)
    u0, u1 = major(add(right0, g0), 1), major(add(left1, g1), -1)
    owned = u0.shape[0] // 2

    def part(rng, *parts):
        return add(*[value[rng] for value in parts])

    first, second = slice(0, owned), slice(owned, 2 * owned)
    n1 = minor(part(second, here0, t0, u0), -1)
    n2 = minor(part(first, here1, t1, u1), 1)
    n3 = minor(part(second, here1, t1, u1), 2)
    return add(*[value[first] for value in (here0, t0, u0)], n1, n2, n3)


def weight_rows_body(starts, size, rows_ref, *refs):
    pieces, (out_ref, sem) = refs[:-2], refs[-2:]
    for i, piece in enumerate(pieces):
        for j in range(piece.shape[0] // size):
            row = pl.multiple_of(rows_ref[starts[i] // size + j], size)
            pltpu.make_async_copy(
                piece.at[pl.ds(j * size, size)], out_ref.at[pl.ds(row, size)], sem
            ).start()
    pltpu.make_async_copy(out_ref, out_ref, sem).wait()


def weight_rows(order, pieces, size):
    starts, depth = [], 0
    for piece in pieces:
        starts.append(depth)
        depth += piece.shape[0]
    width = pieces[0].shape[1]
    hbm = pl.BlockSpec(memory_space=pl.ANY)
    return pl.pallas_call(
        functools.partial(weight_rows_body, tuple(starts), size),
        out_shape=jax.ShapeDtypeStruct((depth, width), BF),
        in_specs=[pl.BlockSpec(memory_space=pltpu.SMEM)] + [hbm] * len(pieces),
        out_specs=pl.BlockSpec(memory_space=pltpu.VMEM),
        scratch_shapes=[pltpu.SemaphoreType.DMA],
        compiler_params=pltpu.CompilerParams(vmem_limit_bytes=VMEM_LIMIT),
        cost_estimate=pl.CostEstimate(
            flops=0, bytes_accessed=4 * depth * width, transcendentals=0
        ),
        name="weight_rows",
    )(order, *pieces)


TN = (((0,), (0,)), ((), ()))
NT = (((1,), (1,)), ((), ()))


def load(pieces, rows_ref, first, size, tok_ref, weight, tok, sems, column):
    parts, start = [], 0
    cols = pl.ds(column, weight.shape[1])
    for i, piece in enumerate(pieces):
        count = piece.shape[0]
        rng = pl.ds(start, count)
        whole = pltpu.make_async_copy(piece.at[:, cols], weight.at[rng], sems.at[0, i])
        whole.start()
        for j in range(count // size):
            row = pl.multiple_of(rows_ref[first + start // size + j], size)
            pltpu.make_async_copy(
                tok_ref.at[pl.ds(row, size)], tok.at[pl.ds(start + j * size, size)], sems.at[1, i]
            ).start()
        waits = (
            whole,
            pltpu.make_async_copy(tok_ref.at[pl.ds(0, count)], tok.at[rng], sems.at[1, i]),
        )
        parts.append((rng, waits))
        start += count
    return parts


def block_dot(pieces, parts, first, count, tok, weight):
    for _, waits in parts[first : first + count]:
        for wait in waits:
            wait.wait()
    start = parts[first][0].start
    rng = slice(start, start + sum(piece.shape[0] for piece in pieces[first : first + count]))
    return lax.dot_general(tok[rng, :], weight[rng, :], TN, preferred_element_type=F32)


def early_body(count, size, rows_ref, tok_ref, *refs):
    pieces, (out_ref, weight, tok, sems) = refs[:count], refs[count:]
    parts = load(pieces, rows_ref, 0, size, tok_ref, weight, tok, sems, 0)
    out_ref[...] = block_dot(pieces, parts, 0, count, tok, weight)


def late_body(first, column, count, size, rows_ref, part_ref, tok_ref, *refs):
    pieces, (out_ref, weight, tok, sems) = refs[:count], refs[count:]
    parts = load(pieces, rows_ref, first, size, tok_ref, weight, tok, sems, column)
    total = part_ref[...] + block_dot(pieces, parts, 0, 4, tok, weight)
    total += block_dot(pieces, parts, 4, count - 4, tok, weight)
    out_ref[...] = total.astype(BF)


def projection(order, size, tok_t, pieces, first, part, column, width, dtype, name):
    rows = tok_t.shape[1]
    depth = sum(piece.shape[0] for piece in pieces)
    smem = pl.BlockSpec(memory_space=pltpu.SMEM)
    hbm = pl.BlockSpec(memory_space=pl.ANY)
    block = column // width
    body = functools.partial(late_body, first, column) if part else early_body
    return pl.pallas_call(
        functools.partial(body, len(pieces), size),
        grid=(1,),
        out_shape=jax.ShapeDtypeStruct((rows, width), dtype),
        in_specs=[smem]
        + [pl.BlockSpec((rows, width), lambda i: (0, block))] * len(part)
        + [hbm] * (1 + len(pieces)),
        out_specs=pl.BlockSpec((rows, width), lambda i: (0, 0)),
        scratch_shapes=[
            pltpu.VMEM((depth, width), BF),
            pltpu.VMEM((depth, rows), BF),
            pltpu.SemaphoreType.DMA((2, len(pieces))),
        ],
        compiler_params=pltpu.CompilerParams(vmem_limit_bytes=VMEM_LIMIT),
        cost_estimate=pl.CostEstimate(
            flops=2 * rows * depth * width,
            bytes_accessed=2 * (rows + width) * depth + 4 * rows * width,
            transcendentals=0,
        ),
        name=name,
    )(order, *part, tok_t, *pieces)


def attention_body(heads, tiles, places_ref, q_ref, kv_ref, out_ref, in_ref, dout_ref,
                   att_ref, dq_ref, own_ref, dout_side_ref, din_side_ref, ext, acc, sem):
    rows = tiles * TILE
    scale = HD ** (-0.5)
    copies = []
    for i, ref in enumerate((out_ref, kv_ref, in_ref)):
        copy = pltpu.make_async_copy(ref, ext.at[pl.ds(i * rows, rows)], sem.at[i])
        copy.start()
        copies.append(copy)
    acc[...] = jnp.zeros_like(acc)
    for copy in copies:
        copy.wait()

    def tile(t, carry):
        here = pl.ds(pl.multiple_of(t * TILE, TILE), TILE)
        window = [
            pl.ds(pl.multiple_of(places_ref[t * WIN + w] * TILE, TILE), TILE) for w in range(WIN)
        ]
        loaded, weights = [], []
        for h in range(heads):
            col = pl.ds(h * HD, HD)
            query = q_ref[here, col]
            dout = dout_ref[here, col]
            keys = jnp.concatenate([ext[rng, pl.ds(2 * h * HD, HD)] for rng in window], axis=0)
            values = jnp.concatenate(
                [ext[rng, pl.ds((2 * h + 1) * HD, HD)] for rng in window], axis=0
            )
            scores = lax.dot_general(keys, query, NT, preferred_element_type=F32) * scale
            dprobs = lax.dot_general(values, dout, NT, preferred_element_type=F32)
            loaded.append((query, dout, keys, values, scores, dprobs))
        for _, _, _, _, scores, dprobs in loaded:
            expo = jnp.exp(scores - jnp.max(scores, axis=0, keepdims=True))
            probs = expo * (1.0 / jnp.sum(expo, axis=0, keepdims=True))
            delta = jnp.sum(probs * dprobs, axis=0, keepdims=True)
            weights.append((probs.astype(BF), (probs * (dprobs - delta) * scale).astype(BF)))
        for h in range(heads):
            col = pl.ds(h * HD, HD)
            query, dout, keys, values, _, _ = loaded[h]
            probs_b, dscores = weights[h]
            att_ref[here, col] = lax.dot_general(
                probs_b, values, TN, preferred_element_type=F32
            ).astype(BF)
            dq_ref[here, col] = lax.dot_general(
                dscores, keys, TN, preferred_element_type=F32
            ).astype(BF)
            dkeys = jnp.dot(dscores, query, preferred_element_type=F32)
            dvalues = jnp.dot(probs_b, dout, preferred_element_type=F32)
            for w, rng in enumerate(window):
                part = slice(w * TILE, (w + 1) * TILE)
                acc[rng, pl.ds(2 * h * HD, HD)] += dkeys[part]
                acc[rng, pl.ds((2 * h + 1) * HD, HD)] += dvalues[part]
        return carry

    lax.fori_loop(0, tiles, tile, 0)
    dout_side_ref[...] = acc[pl.ds(0, rows)].astype(BF)
    own_ref[...] = acc[pl.ds(rows, rows)]
    din_side_ref[...] = acc[pl.ds(2 * rows, rows)].astype(BF)


def attention(places, query, kv, out_side, in_side, grad_out, first):
    rows, width = kv.shape[0], kv.shape[1] // 2
    heads, tiles = width // HD, rows // TILE
    block = first // heads
    part = pl.BlockSpec((rows, width), lambda i: (0, block))
    vmem = pl.BlockSpec(memory_space=pltpu.VMEM)
    hbm = pl.BlockSpec(memory_space=pl.ANY)
    return pl.pallas_call(
        functools.partial(attention_body, heads, tiles),
        grid=(1,),
        out_shape=[
            jax.ShapeDtypeStruct((rows, width), BF),
            jax.ShapeDtypeStruct((rows, width), BF),
            jax.ShapeDtypeStruct((rows, 2 * width), F32),
            jax.ShapeDtypeStruct((rows, 2 * width), BF),
            jax.ShapeDtypeStruct((rows, 2 * width), BF),
        ],
        in_specs=[pl.BlockSpec(memory_space=pltpu.SMEM), part, hbm, hbm, hbm, part],
        out_specs=[pl.BlockSpec((rows, cols), lambda i: (0, 0)) for cols in (width, width, 2 * width, 2 * width, 2 * width)],
        scratch_shapes=[
            pltpu.VMEM((3 * rows, 2 * width), BF),
            pltpu.VMEM((3 * rows, 2 * width), F32),
            pltpu.SemaphoreType.DMA((3,)),
        ],
        compiler_params=pltpu.CompilerParams(vmem_limit_bytes=VMEM_SMALL),
        cost_estimate=pl.CostEstimate(
            flops=24 * rows * WIN * TILE * width,
            bytes_accessed=24 * rows * width,
            transcendentals=rows * WIN * TILE * heads,
        ),
        name="attention",
    )(places, query, kv, out_side, in_side, grad_out)


def weight_grad_body(size, rows_ref, tok_ref, tok_other_ref, *refs):
    blocks, outs = refs[:4], refs[4:12]
    tok, joined, held, sems_in, sems, sems_out = refs[12:]
    tokens = tok_ref.shape[1]
    cut = blocks[0].shape[1]
    loads = []
    for i, block in enumerate(blocks):
        cols = pl.ds(0, cut) if i % 2 == 0 else pl.ds(cut, joined.shape[1] - cut)
        target = joined.at[pl.ds(i // 2 * tokens, tokens), cols]
        loads.append(pltpu.make_async_copy(block, target, sems_in.at[i]))
    for load_ in loads:
        load_.start()
    places = [8 * group + i for group in range(4) for i in range(4)]
    sides = (tok_ref, tok_other_ref)
    for k, side in enumerate(sides):
        cols = pl.ds(k * tokens, tokens)
        for j, i in enumerate(places):
            row = pl.multiple_of(rows_ref[i], size)
            pltpu.make_async_copy(
                side.at[pl.ds(row, size)], tok.at[pl.ds(j * size, size), cols], sems.at[k]
            ).start()
    for k, side in enumerate(sides):
        target = tok.at[:, pl.ds(k * tokens, tokens)]
        pltpu.make_async_copy(side.at[pl.ds(0, tok.shape[0])], target, sems.at[k]).wait()
    for load_ in loads:
        load_.wait()
    held[...] = jnp.dot(tok[...], joined[...], preferred_element_type=F32).astype(BF)
    stores = []
    for i, out in enumerate(outs):
        rows = out.shape[0]
        stores.append(
            pltpu.make_async_copy(held.at[pl.ds(i * rows, rows)], out, sems_out.at[i])
        )
        stores[-1].start()
    for store in stores:
        store.wait()


def weight_grad(order, tok_t, tok_other, own, other, size):
    tokens = tok_t.shape[1]
    width = own[0].shape[1] + own[1].shape[1]
    depth = tok_other.shape[0] // 2
    hbm = pl.BlockSpec(memory_space=pl.ANY)
    outs = pl.pallas_call(
        functools.partial(weight_grad_body, size),
        out_shape=[jax.ShapeDtypeStruct((depth // 8, width), BF)] * 8,
        in_specs=[pl.BlockSpec(memory_space=pltpu.SMEM)] + [hbm] * 6,
        out_specs=[hbm] * 8,
        scratch_shapes=[
            pltpu.VMEM((depth, 2 * tokens), BF),
            pltpu.VMEM((2 * tokens, width), BF),
            pltpu.VMEM((depth, width), BF),
            pltpu.SemaphoreType.DMA((4,)),
            pltpu.SemaphoreType.DMA((2,)),
            pltpu.SemaphoreType.DMA((8,)),
        ],
        compiler_params=pltpu.CompilerParams(vmem_limit_bytes=VMEM_LIMIT),
        cost_estimate=pl.CostEstimate(
            flops=4 * depth * tokens * width,
            bytes_accessed=2 * (2 * depth * tokens + depth * width),
            transcendentals=0,
        ),
        name="weight_grad",
    )(order, tok_t, tok_other, *own, *other)
    return [outs[i : i + 2] for i in range(0, 8, 2)]


def input_grad_body(shared, chunks, which_ref, *refs):
    blocks, w_ref, outs = refs[:4], refs[4], refs[5:-6]
    joined, weight, held, sems_in, sems, sems_out = refs[-6:]
    rows, chunk = held.shape[1:]
    cut = blocks[0].shape[1]
    loads = []
    for i, block in enumerate(blocks):
        cols = pl.ds(0, cut) if i % 2 == 0 else pl.ds(cut, joined.shape[1] - cut)
        target = joined.at[pl.ds(i // 2 * rows, rows), cols]
        loads.append(pltpu.make_async_copy(block, target, sems_in.at[i]))
        loads[-1].start()
    weights = []
    for i in range(chunks):
        first = pl.multiple_of(which_ref[i] * chunk, chunk)
        weights.append(
            pltpu.make_async_copy(
                w_ref.at[pl.ds(first, chunk)], weight.at[pl.ds(i * chunk, chunk)], sems.at[i]
            )
        )
        weights[-1].start()
    for load_ in loads:
        load_.wait()
    stores = []

    def store(value):
        at = len(stores)
        held[at] = value
        stores.append(pltpu.make_async_copy(held.at[at], outs[at], sems_out.at[at]))
        stores[-1].start()

    for i in range(shared):
        weights[i].wait()
        total = lax.dot_general(
            weight[i * chunk : (i + 1) * chunk, :], joined[...], NT, preferred_element_type=F32
        )
        total = total.astype(BF).T
        store(total[:rows])
        store(total[rows:])
    for i in range(shared, chunks):
        weights[i].wait()
    total = lax.dot_general(
        weight[shared * chunk :, :], joined[:rows, :], NT, preferred_element_type=F32
    )
    total = total.astype(BF).T
    for i in range(chunks - shared):
        store(total[:, i * chunk : (i + 1) * chunk])
    for store_ in stores:
        store_.wait()


def input_grad(which, shared, own, other, whole, parts):
    rows, width = own[0].shape[0], whole.shape[1]
    chunk, chunks = whole.shape[0] // parts, which.shape[0]
    count = chunks + shared
    hbm = pl.BlockSpec(memory_space=pl.ANY)
    return pl.pallas_call(
        functools.partial(input_grad_body, shared, chunks),
        out_shape=[jax.ShapeDtypeStruct((rows, chunk), BF)] * count,
        in_specs=[pl.BlockSpec(memory_space=pltpu.SMEM)] + [hbm] * 5,
        out_specs=[hbm] * count,
        scratch_shapes=[
            pltpu.VMEM((2 * rows, width), BF),
            pltpu.VMEM((chunks * chunk, width), BF),
            pltpu.VMEM((count, rows, chunk), BF),
            pltpu.SemaphoreType.DMA((4,)),
            pltpu.SemaphoreType.DMA((chunks,)),
            pltpu.SemaphoreType.DMA((count,)),
        ],
        compiler_params=pltpu.CompilerParams(vmem_limit_bytes=VMEM_LIMIT),
        cost_estimate=pl.CostEstimate(
            flops=2 * count * rows * chunk * width,
            bytes_accessed=2 * (chunks * chunk * width + count * rows * chunk),
            transcendentals=0,
        ),
        name="input_grad",
    )(which, *own, *other, whole)


def sum_heads(own, other, whole, c, between):
    peers = lax.axis_size("head")
    me = lax.axis_index("head")
    steps = jnp.array([3, 2, 1, peers // 2, 0], jnp.int32)
    which = (me + (1 - 2 * c) * steps) % peers
    own3, other3, own2, other2, own1, other1, far, mine = input_grad(
        which.astype(jnp.int32), 3, own, other, whole, peers
    )
    far = ring_heads(far)
    other3 = ring_heads(other3)
    result, own3 = between(mine, own3)
    own3 = ring_heads(add(own3, far))
    rows = own3.shape[0]
    two = jnp.concatenate([add(own2, own3), add(other2, other3)], axis=0)
    two = ring_heads(two)
    one = jnp.concatenate([add(own1, two[:rows]), add(other1, two[rows:])], axis=0)
    one = ring_heads(one)
    return add(mine, one[:rows], swap(one[rows:])), result


def shards(tokens, weight, grad_out, neighbours):
    rows, depth = tokens.shape
    owned, heads = weight.shape[:2]
    size = owned // 2
    tiles = rows // TILE
    tiles_all = tiles * lax.axis_size("space")
    index = lax.axis_index("space")
    c, x, y = index % 2, (index // 2) % NX, index // (2 * NX)

    split = weight.reshape(owned, heads, 3, HD)
    flat = jnp.concatenate(
        [split[:, :, 1:].reshape(owned, -1), split[:, :, 0].reshape(owned, -1)], axis=1
    )
    order = block_order(y, x, c, owned)
    width = flat.shape[1]

    def project_early(tok_t, pieces):
        return projection(order, owned, tok_t, pieces, 0, (), 0, width, F32, "project_early")

    tok_t, part, early, late = gather_rows(flat, tokens.T, project_early)
    first = sum(piece.shape[0] for piece in early) // owned
    cut = 2 * heads * HD
    kv = projection(order, owned, tok_t, late, first, (part,), 0, cut, BF, "project_kv")
    out_side, in_side = outside(kv), swap(kv)
    query = projection(
        order, owned, tok_t, late, first, (part,), cut, width - cut, BF, "project_q"
    )

    places = (neighbours - (index - 1) * tiles) % tiles_all
    block = places // tiles
    places = (jnp.where(c == 0, block, 2 - block) * tiles + places % tiles).reshape(-1)
    out_side, query = lax.optimization_barrier((out_side, query))
    tok_other = swap(lax.optimization_barrier((tok_t, out_side))[0])
    attended, dq, dkv, dout_side, din_side = attention(
        places, query, kv, out_side, in_side, grad_out, 0
    )
    pieces, dq = lax.optimization_barrier((early + late, dq))
    whole = weight_rows(order, pieces, owned)
    from_out, whole = lax.optimization_barrier((outside(dout_side), whole))
    dkv = add(dkv, from_out, swap(din_side))
    own, other = (dkv, dq), (swap(dkv), swap(dq))

    def between(before, waiting):
        tied = lax.optimization_barrier((own, before))[0]
        grads = weight_grad(order, tok_t, tok_other, tied, other, owned)
        return lax.optimization_barrier((grads, waiting))

    grad_input, grads = sum_heads(own, other, whole, c, between)
    mine = scatter_rows(*grads)
    grad_weight = jnp.concatenate(
        [
            mine[:, cut:].reshape(owned, heads, 1, HD),
            mine[:, :cut].reshape(owned, heads, 2, HD),
        ],
        axis=2,
    ).reshape(weight.shape)
    return (attended, grad_input, grad_weight)


def solution(mesh):
    return jax.shard_map(
        shards,
        mesh=mesh,
        in_specs=(P("space", None), P("space", "head", None), P("space", "head"), P("space", None)),
        out_specs=(P("space", "head"), P("space", "head"), P("space", "head", None)),
        check_vma=False,
    )
```

```python
import functools

import jax
import jax.numpy as jnp
from jax import lax
from jax.experimental import pallas as pl
from jax.experimental.pallas import tpu as pltpu
from jax.sharding import PartitionSpec as P

HD = 128
TILE = 128
WIN = 4
NX = 4
NY = 4
BF = jnp.bfloat16
F32 = jnp.float32
VMEM_LIMIT = 56 * 1024 * 1024
VMEM_SMALL = 28 * 1024 * 1024


def space_perm(move):
    pairs = []
    for y in range(NY):
        for x in range(NX):
            for c in range(2):
                to_y, to_x, to_c = move(y, x, c)
                pairs.append(((y * NX + x) * 2 + c, (to_y % NY * NX + to_x % NX) * 2 + to_c))
    return pairs


def permute(value, move):
    return lax.ppermute(value, "space", space_perm(move))


def swap(value):
    return permute(value, lambda y, x, c: (y, x, 1 - c))


def minor(value, by):
    return permute(value, lambda y, x, c: (y + by * c, x + by * (1 - c), c))


def major(value, by):
    return permute(value, lambda y, x, c: (y + by * (1 - c), x + by * c, c))


def outside(value):
    peers = lax.axis_size("space")
    return lax.ppermute(
        value, "space", [(i, (i + 1 if i % 2 else i - 1) % peers) for i in range(peers)]
    )


NEAR = (0, -1, 1, 2)


def ring_heads(value):
    space, peers = lax.axis_size("space"), lax.axis_size("head")
    pairs = []
    for i in range(space):
        for j in range(peers):
            pairs.append((i * peers + j, i * peers + (j + 1 - 2 * (i % 2)) % peers))
    return lax.ppermute(value, ("space", "head"), pairs)


GROUPS = (((0, 0), (0, 1)), ((-1, 0), (1, 1)), ((-1, 1), (1, 0)), ((2, 0), (2, 1)))


def block_order(y, x, c, owned):
    rows = []
    for group in GROUPS:
        for core in (c, 1 - c):
            for p, half in group:
                for q in NEAR[2 * half : 2 * half + 2]:
                    dy = jnp.where(core == 0, p, q)
                    dx = jnp.where(core == 0, q, p)
                    rows.append(((((y + dy) % NY) * NX + (x + dx) % NX) * 2 + core) * owned)
    return jnp.stack(rows).astype(jnp.int32)


def gather_rows(shard, tok_t):
    h0 = jnp.concatenate([shard, minor(shard, 1)], axis=0)
    h1 = jnp.concatenate([minor(shard, -1), minor(shard, 2)], axis=0)
    r0, l1 = major(h0, 1), major(h1, -1)
    r1, l0 = major(h1, 1), major(h0, -1)
    near = jnp.concatenate([h0, h1], axis=0)
    f0, f1 = major(r0, 1), major(l1, -1)
    f0, f1, tok_t = lax.optimization_barrier((f0, f1, tok_t))
    pieces = [near, swap(near)]
    r0, l1, r1, l0 = lax.optimization_barrier((r0, l1, r1, l0))
    pieces += [r0, l1, swap(r0), swap(l1), r1, l0, swap(r1), swap(l0), f0, f1, swap(f0), swap(f1)]
    return tok_t, pieces


def add(*parts):
    return sum(part.astype(F32) for part in parts).astype(BF)


def scatter_rows(here, first, second, far):
    here0, here1 = here
    left0, right1 = first
    left1, right0 = second
    g0, g1 = major(far[0], 1), major(far[1], -1)
    t0, t1 = major(left0, -1), major(right1, 1)
    u0, u1 = major(add(right0, g0), 1), major(add(left1, g1), -1)
    owned = u0.shape[0] // 2

    def part(rng, *parts):
        return add(*[value[rng] for value in parts])

    first, second = slice(0, owned), slice(owned, 2 * owned)
    n1 = minor(part(second, here0, t0, u0), -1)
    n2 = minor(part(first, here1, t1, u1), 1)
    n3 = minor(part(second, here1, t1, u1), 2)
    return add(*[value[first] for value in (here0, t0, u0)], n1, n2, n3)


def weight_rows_body(starts, size, rows_ref, *refs):
    pieces, (out_ref, sem) = refs[:-2], refs[-2:]
    for i, piece in enumerate(pieces):
        for j in range(piece.shape[0] // size):
            row = pl.multiple_of(rows_ref[starts[i] // size + j], size)
            pltpu.make_async_copy(
                piece.at[pl.ds(j * size, size)], out_ref.at[pl.ds(row, size)], sem
            ).start()
    pltpu.make_async_copy(out_ref, out_ref, sem).wait()


def weight_rows(order, pieces, size):
    starts, depth = [], 0
    for piece in pieces:
        starts.append(depth)
        depth += piece.shape[0]
    width = pieces[0].shape[1]
    hbm = pl.BlockSpec(memory_space=pl.ANY)
    return pl.pallas_call(
        functools.partial(weight_rows_body, tuple(starts), size),
        out_shape=jax.ShapeDtypeStruct((depth, width), BF),
        in_specs=[pl.BlockSpec(memory_space=pltpu.SMEM)] + [hbm] * len(pieces),
        out_specs=pl.BlockSpec(memory_space=pltpu.VMEM),
        scratch_shapes=[pltpu.SemaphoreType.DMA],
        compiler_params=pltpu.CompilerParams(vmem_limit_bytes=VMEM_LIMIT),
        cost_estimate=pl.CostEstimate(
            flops=0, bytes_accessed=4 * depth * width, transcendentals=0
        ),
        name="weight_rows",
    )(order, *pieces)


TN = (((0,), (0,)), ((), ()))
NT = (((1,), (1,)), ((), ()))


def project_body(column, count, size, rows_ref, tok_ref, *refs):
    pieces, (out_ref, weight, tok, sems) = refs[:count], refs[count:]
    cols = pl.ds(column, weight.shape[1])
    depth = weight.shape[0]
    waits, start = [], 0
    for i, piece in enumerate(pieces):
        rows = piece.shape[0]
        rng = pl.ds(start, rows)
        waits.append((start, pltpu.make_async_copy(piece.at[:, cols], weight.at[rng], sems.at[0, i])))
        waits[-1][1].start()
        for j in range(rows // size):
            row = pl.multiple_of(rows_ref[start // size + j], size)
            pltpu.make_async_copy(
                tok_ref.at[pl.ds(row, size)], tok.at[pl.ds(start + j * size, size)], sems.at[1, i]
            ).start()
        waits.append(
            (start, pltpu.make_async_copy(tok_ref.at[pl.ds(0, rows)], tok.at[rng], sems.at[1, i]))
        )
        start += rows
    total = None
    for part in range(2):
        for at, wait in waits:
            if at * 2 // depth == part:
                wait.wait()
        rng = slice(part * depth // 2, (part + 1) * depth // 2)
        term = lax.dot_general(tok[rng, :], weight[rng, :], TN, preferred_element_type=F32)
        total = term if total is None else total + term
    out_ref[...] = total.astype(BF)


def project(order, size, tok_t, pieces, column, width, name):
    rows = tok_t.shape[1]
    depth = sum(piece.shape[0] for piece in pieces)
    hbm = pl.BlockSpec(memory_space=pl.ANY)
    return pl.pallas_call(
        functools.partial(project_body, column, len(pieces), size),
        grid=(1,),
        out_shape=jax.ShapeDtypeStruct((rows, width), BF),
        in_specs=[pl.BlockSpec(memory_space=pltpu.SMEM)] + [hbm] * (1 + len(pieces)),
        out_specs=pl.BlockSpec((rows, width), lambda i: (0, 0)),
        scratch_shapes=[
            pltpu.VMEM((depth, width), BF),
            pltpu.VMEM((depth, rows), BF),
            pltpu.SemaphoreType.DMA((2, len(pieces))),
        ],
        compiler_params=pltpu.CompilerParams(vmem_limit_bytes=VMEM_LIMIT),
        cost_estimate=pl.CostEstimate(
            flops=2 * rows * depth * width,
            bytes_accessed=2 * (rows + width) * depth + 2 * rows * width,
            transcendentals=0,
        ),
        name=name,
    )(order, tok_t, *pieces)


def attention_body(heads, tiles, places_ref, q_ref, kv_ref, out_ref, in_ref, dout_ref,
                   att_ref, dq_ref, own_ref, dout_side_ref, din_side_ref, ext, acc, sem):
    rows = tiles * TILE
    scale = HD ** (-0.5)
    copies = []
    for i, ref in enumerate((out_ref, kv_ref, in_ref)):
        copy = pltpu.make_async_copy(ref, ext.at[pl.ds(i * rows, rows)], sem.at[i])
        copy.start()
        copies.append(copy)
    acc[...] = jnp.zeros_like(acc)
    for copy in copies:
        copy.wait()

    def tile(t, carry):
        here = pl.ds(pl.multiple_of(t * TILE, TILE), TILE)
        window = [
            pl.ds(pl.multiple_of(places_ref[t * WIN + w] * TILE, TILE), TILE) for w in range(WIN)
        ]
        loaded, weights = [], []
        for h in range(heads):
            col = pl.ds(h * HD, HD)
            query = q_ref[here, col]
            dout = dout_ref[here, col]
            keys = jnp.concatenate([ext[rng, pl.ds(2 * h * HD, HD)] for rng in window], axis=0)
            values = jnp.concatenate(
                [ext[rng, pl.ds((2 * h + 1) * HD, HD)] for rng in window], axis=0
            )
            scores = lax.dot_general(keys, query, NT, preferred_element_type=F32) * scale
            dprobs = lax.dot_general(values, dout, NT, preferred_element_type=F32)
            loaded.append((query, dout, keys, values, scores, dprobs))
        for _, _, _, _, scores, dprobs in loaded:
            expo = jnp.exp(scores - jnp.max(scores, axis=0, keepdims=True))
            probs = expo * (1.0 / jnp.sum(expo, axis=0, keepdims=True))
            delta = jnp.sum(probs * dprobs, axis=0, keepdims=True)
            weights.append((probs.astype(BF), (probs * (dprobs - delta) * scale).astype(BF)))
        for h in range(heads):
            col = pl.ds(h * HD, HD)
            query, dout, keys, values, _, _ = loaded[h]
            probs_b, dscores = weights[h]
            att_ref[here, col] = lax.dot_general(
                probs_b, values, TN, preferred_element_type=F32
            ).astype(BF)
            dq_ref[here, col] = lax.dot_general(
                dscores, keys, TN, preferred_element_type=F32
            ).astype(BF)
            dkeys = jnp.dot(dscores, query, preferred_element_type=F32)
            dvalues = jnp.dot(probs_b, dout, preferred_element_type=F32)
            for w, rng in enumerate(window):
                part = slice(w * TILE, (w + 1) * TILE)
                acc[rng, pl.ds(2 * h * HD, HD)] += dkeys[part]
                acc[rng, pl.ds((2 * h + 1) * HD, HD)] += dvalues[part]
        return carry

    lax.fori_loop(0, tiles, tile, 0)
    dout_side_ref[...] = acc[pl.ds(0, rows)].astype(BF)
    own_ref[...] = acc[pl.ds(rows, rows)]
    din_side_ref[...] = acc[pl.ds(2 * rows, rows)].astype(BF)


def attention(places, query, kv, out_side, in_side, grad_out, first):
    rows, width = kv.shape[0], kv.shape[1] // 2
    heads, tiles = width // HD, rows // TILE
    block = first // heads
    part = pl.BlockSpec((rows, width), lambda i: (0, block))
    vmem = pl.BlockSpec(memory_space=pltpu.VMEM)
    hbm = pl.BlockSpec(memory_space=pl.ANY)
    return pl.pallas_call(
        functools.partial(attention_body, heads, tiles),
        grid=(1,),
        out_shape=[
            jax.ShapeDtypeStruct((rows, width), BF),
            jax.ShapeDtypeStruct((rows, width), BF),
            jax.ShapeDtypeStruct((rows, 2 * width), F32),
            jax.ShapeDtypeStruct((rows, 2 * width), BF),
            jax.ShapeDtypeStruct((rows, 2 * width), BF),
        ],
        in_specs=[pl.BlockSpec(memory_space=pltpu.SMEM), part, hbm, hbm, hbm, part],
        out_specs=[pl.BlockSpec((rows, cols), lambda i: (0, 0)) for cols in (width, width, 2 * width, 2 * width, 2 * width)],
        scratch_shapes=[
            pltpu.VMEM((3 * rows, 2 * width), BF),
            pltpu.VMEM((3 * rows, 2 * width), F32),
            pltpu.SemaphoreType.DMA((3,)),
        ],
        compiler_params=pltpu.CompilerParams(vmem_limit_bytes=VMEM_SMALL),
        cost_estimate=pl.CostEstimate(
            flops=24 * rows * WIN * TILE * width,
            bytes_accessed=24 * rows * width,
            transcendentals=rows * WIN * TILE * heads,
        ),
        name="attention",
    )(places, query, kv, out_side, in_side, grad_out)


def weight_grad_body(size, rows_ref, tok_ref, tok_other_ref, *refs):
    blocks, outs = refs[:4], refs[4:12]
    tok, joined, held, sems_in, sems, sems_out = refs[12:]
    tokens = tok_ref.shape[1]
    cut = blocks[0].shape[1]
    loads = []
    for i, block in enumerate(blocks):
        cols = pl.ds(0, cut) if i % 2 == 0 else pl.ds(cut, joined.shape[1] - cut)
        target = joined.at[pl.ds(i // 2 * tokens, tokens), cols]
        loads.append(pltpu.make_async_copy(block, target, sems_in.at[i]))
    for load_ in loads:
        load_.start()
    places = [8 * group + i for group in range(4) for i in range(4)]
    sides = (tok_ref, tok_other_ref)
    for k, side in enumerate(sides):
        cols = pl.ds(k * tokens, tokens)
        for j, i in enumerate(places):
            row = pl.multiple_of(rows_ref[i], size)
            pltpu.make_async_copy(
                side.at[pl.ds(row, size)], tok.at[pl.ds(j * size, size), cols], sems.at[k]
            ).start()
    for k, side in enumerate(sides):
        target = tok.at[:, pl.ds(k * tokens, tokens)]
        pltpu.make_async_copy(side.at[pl.ds(0, tok.shape[0])], target, sems.at[k]).wait()
    for load_ in loads:
        load_.wait()
    held[...] = jnp.dot(tok[...], joined[...], preferred_element_type=F32).astype(BF)
    stores = []
    for i, out in enumerate(outs):
        rows = out.shape[0]
        stores.append(
            pltpu.make_async_copy(held.at[pl.ds(i * rows, rows)], out, sems_out.at[i])
        )
        stores[-1].start()
    for store in stores:
        store.wait()


def weight_grad(order, tok_t, tok_other, own, other, size):
    tokens = tok_t.shape[1]
    width = own[0].shape[1] + own[1].shape[1]
    depth = tok_other.shape[0] // 2
    hbm = pl.BlockSpec(memory_space=pl.ANY)
    outs = pl.pallas_call(
        functools.partial(weight_grad_body, size),
        out_shape=[jax.ShapeDtypeStruct((depth // 8, width), BF)] * 8,
        in_specs=[pl.BlockSpec(memory_space=pltpu.SMEM)] + [hbm] * 6,
        out_specs=[hbm] * 8,
        scratch_shapes=[
            pltpu.VMEM((depth, 2 * tokens), BF),
            pltpu.VMEM((2 * tokens, width), BF),
            pltpu.VMEM((depth, width), BF),
            pltpu.SemaphoreType.DMA((4,)),
            pltpu.SemaphoreType.DMA((2,)),
            pltpu.SemaphoreType.DMA((8,)),
        ],
        compiler_params=pltpu.CompilerParams(vmem_limit_bytes=VMEM_LIMIT),
        cost_estimate=pl.CostEstimate(
            flops=4 * depth * tokens * width,
            bytes_accessed=2 * (2 * depth * tokens + depth * width),
            transcendentals=0,
        ),
        name="weight_grad",
    )(order, tok_t, tok_other, *own, *other)
    return [outs[i : i + 2] for i in range(0, 8, 2)]


def input_grad_body(shared, chunks, which_ref, *refs):
    blocks, w_ref, outs = refs[:4], refs[4], refs[5:-6]
    joined, weight, held, sems_in, sems, sems_out = refs[-6:]
    rows, chunk = held.shape[1:]
    cut = blocks[0].shape[1]
    loads = []
    for i, block in enumerate(blocks):
        cols = pl.ds(0, cut) if i % 2 == 0 else pl.ds(cut, joined.shape[1] - cut)
        target = joined.at[pl.ds(i // 2 * rows, rows), cols]
        loads.append(pltpu.make_async_copy(block, target, sems_in.at[i]))
        loads[-1].start()
    weights = []
    for i in range(chunks):
        first = pl.multiple_of(which_ref[i] * chunk, chunk)
        weights.append(
            pltpu.make_async_copy(
                w_ref.at[pl.ds(first, chunk)], weight.at[pl.ds(i * chunk, chunk)], sems.at[i]
            )
        )
        weights[-1].start()
    for load_ in loads:
        load_.wait()
    stores = []

    def store(value):
        at = len(stores)
        held[at] = value
        stores.append(pltpu.make_async_copy(held.at[at], outs[at], sems_out.at[at]))
        stores[-1].start()

    for i in range(shared):
        weights[i].wait()
        total = lax.dot_general(
            weight[i * chunk : (i + 1) * chunk, :], joined[...], NT, preferred_element_type=F32
        )
        total = total.astype(BF).T
        store(total[:rows])
        store(total[rows:])
    for i in range(shared, chunks):
        weights[i].wait()
    total = lax.dot_general(
        weight[shared * chunk :, :], joined[:rows, :], NT, preferred_element_type=F32
    )
    total = total.astype(BF).T
    for i in range(chunks - shared):
        store(total[:, i * chunk : (i + 1) * chunk])
    for store_ in stores:
        store_.wait()


def input_grad(which, shared, own, other, whole, parts):
    rows, width = own[0].shape[0], whole.shape[1]
    chunk, chunks = whole.shape[0] // parts, which.shape[0]
    count = chunks + shared
    hbm = pl.BlockSpec(memory_space=pl.ANY)
    return pl.pallas_call(
        functools.partial(input_grad_body, shared, chunks),
        out_shape=[jax.ShapeDtypeStruct((rows, chunk), BF)] * count,
        in_specs=[pl.BlockSpec(memory_space=pltpu.SMEM)] + [hbm] * 5,
        out_specs=[hbm] * count,
        scratch_shapes=[
            pltpu.VMEM((2 * rows, width), BF),
            pltpu.VMEM((chunks * chunk, width), BF),
            pltpu.VMEM((count, rows, chunk), BF),
            pltpu.SemaphoreType.DMA((4,)),
            pltpu.SemaphoreType.DMA((chunks,)),
            pltpu.SemaphoreType.DMA((count,)),
        ],
        compiler_params=pltpu.CompilerParams(vmem_limit_bytes=VMEM_LIMIT),
        cost_estimate=pl.CostEstimate(
            flops=2 * count * rows * chunk * width,
            bytes_accessed=2 * (chunks * chunk * width + count * rows * chunk),
            transcendentals=0,
        ),
        name="input_grad",
    )(which, *own, *other, whole)


def sum_heads(own, other, whole, c, between):
    peers = lax.axis_size("head")
    me = lax.axis_index("head")
    steps = jnp.array([3, 2, 1, peers // 2, 0], jnp.int32)
    which = (me + (1 - 2 * c) * steps) % peers
    own3, other3, own2, other2, own1, other1, far, mine = input_grad(
        which.astype(jnp.int32), 3, own, other, whole, peers
    )
    far = ring_heads(far)
    other3 = ring_heads(other3)
    result, own3 = between(mine, own3)
    own3 = ring_heads(add(own3, far))
    rows = own3.shape[0]
    other2 = ring_heads(add(other2, other3))
    own2 = ring_heads(add(own2, own3))
    one = jnp.concatenate([add(own1, own2), add(other1, other2)], axis=0)
    one = ring_heads(one)
    return add(mine, one[:rows], swap(one[rows:])), result


def shards(tokens, weight, grad_out, neighbours):
    rows, depth = tokens.shape
    owned, heads = weight.shape[:2]
    size = owned // 2
    tiles = rows // TILE
    tiles_all = tiles * lax.axis_size("space")
    index = lax.axis_index("space")
    c, x, y = index % 2, (index // 2) % NX, index // (2 * NX)

    split = weight.reshape(owned, heads, 3, HD)
    flat = jnp.concatenate(
        [split[:, :, 1:].reshape(owned, -1), split[:, :, 0].reshape(owned, -1)], axis=1
    )
    order = block_order(y, x, c, owned)
    width = flat.shape[1]

    tok_t, pieces = gather_rows(flat, tokens.T)
    cut = 2 * heads * HD
    kv = project(order, owned, tok_t, pieces, 0, cut, "project_kv")
    out_side, in_side = outside(kv), swap(kv)
    query = project(order, owned, tok_t, pieces, cut, width - cut, "project_q")

    places = (neighbours - (index - 1) * tiles) % tiles_all
    block = places // tiles
    places = (jnp.where(c == 0, block, 2 - block) * tiles + places % tiles).reshape(-1)
    out_side, query = lax.optimization_barrier((out_side, query))
    tok_other = swap(lax.optimization_barrier((tok_t, out_side))[0])
    attended, dq, dkv, dout_side, din_side = attention(
        places, query, kv, out_side, in_side, grad_out, 0
    )
    pieces, dq = lax.optimization_barrier((pieces, dq))
    whole = weight_rows(order, pieces, owned)
    from_out, whole = lax.optimization_barrier((outside(dout_side), whole))
    dkv = add(dkv, from_out, swap(din_side))
    own, other = (dkv, dq), (swap(dkv), swap(dq))

    def between(before, waiting):
        tied = lax.optimization_barrier((own, before))[0]
        grads = weight_grad(order, tok_t, tok_other, tied, other, owned)
        return lax.optimization_barrier((grads, waiting))

    grad_input, grads = sum_heads(own, other, whole, c, between)
    mine = scatter_rows(*grads)
    grad_weight = jnp.concatenate(
        [
            mine[:, cut:].reshape(owned, heads, 1, HD),
            mine[:, :cut].reshape(owned, heads, 2, HD),
        ],
        axis=2,
    ).reshape(weight.shape)
    return (attended, grad_input, grad_weight)


def solution(mesh):
    return jax.shard_map(
        shards,
        mesh=mesh,
        in_specs=(P("space", None), P("space", "head", None), P("space", "head"), P("space", None)),
        out_specs=(P("space", "head"), P("space", "head"), P("space", "head", None)),
        check_vma=False,
    )
```
